32 devices in a mesh: row: 4 (over x, core), col: 8 (over z, y).
Axes of the slice: x: 2, y: 2, z: 4, core: 2. Of those that a mesh axis runs over, the one named last changes fastest.
Arguments:
- leaf_rhs: bfloat16 [768, 128, 512], P(('row', 'col')), may hold values from -6 to 6
- leaf_inverse: bfloat16 [768, 128, 128], P(('row', 'col')), as said below
- leaf_link: bfloat16 [768, 128, 128], P(('row', 'col')), may hold values from -0.109375 to 0.109375
- leaf_parent: int32 [768], P(('row', 'col')), may hold values from 0 to 31, as said below
- node_rhs: bfloat16 [32, 128, 512], P(('row', 'col')), may hold values from -6 to 6
- node_inverse: bfloat16 [32, 128, 128], P(('row', 'col')), as said below
- node_link: bfloat16 [32, 128, 128], P(('row', 'col')), may hold values from -0.5 to 0.5
- node_parent: int32 [32], P('row'), may hold values from 0 to 31, as said below
- middle_rhs: bfloat16 [32, 128, 512], P('row'), may hold values from -6 to 6
- middle_inverse: bfloat16 [32, 128, 128], P('row'), as said below
- middle_link: bfloat16 [32, 128, 128], P('row'), may hold values from -0.1875 to 0.1875
- middle_parent: int32 [32], P('row'), may hold values from 0 to 3
- top_rhs: bfloat16 [4, 128, 512], replicated, may hold values from -6 to 6
- top_inverse: bfloat16 [4, 128, 128], replicated, as said below
Outputs:
- leaf_result: bfloat16 [768, 128, 512], P(('row', 'col'))
- node_result: bfloat16 [32, 128, 512], P(('row', 'col'))
- middle_result: bfloat16 [32, 128, 512], P('row')
- top_result: bfloat16 [4, 128, 512], replicated
The draws below stay inside these ranges and needn't reach their ends.
Inputs may be any that keep to these rules, and one draw needn't show every extreme that they name: `leaf_parent`: the parent of a leaf held by the device at grid row r lies in block row r: it is r * 8 + c for some c below 8. `node_parent`: the parent of second-level supernode r * 8 + c is r * 8 + j for some j below 8. `leaf_inverse`: each block is lower triangular. `node_inverse`: each block is lower triangular. `middle_inverse`: each block is lower triangular. `top_inverse`: each block is lower triangular.
All inputs are finite; a program needn't handle non-finite values.
Results may differ from the reference program's by a relative error of at most 0.017.
Values may be sent and summed in bfloat16 or wider, within the bound.
A program may use at most 128 MiB of HBM per device.

```python
import jax
import jax.numpy as jnp
from jax import lax

W = 128
R = 512
LEAF_DEV = 24
K2 = 8
K3 = 4
PEERS = 8
NODES = 32
LEAVES = 768
MIDDLE = 32


def draw_inverse(key, count):
    lower_key, diag_key = jax.random.split(key)
    lower = jax.random.normal(lower_key, (count, W, W), jnp.float32) * W ** (-0.5)
    diagonal = jax.random.uniform(diag_key, (count, W), jnp.float32, 0.7, 1.3)
    strict = jnp.tril(jnp.ones((W, W), jnp.float32), -1)
    identity = jnp.eye(W, dtype=jnp.float32)
    return (lower * strict + identity * diagonal[:, None, :]).astype(jnp.bfloat16)


def draw_leaf_inverse(key, part):
    return draw_inverse(jax.random.fold_in(key, 11), LEAVES)


def draw_node_inverse(key, part):
    return draw_inverse(jax.random.fold_in(key, 12), NODES)


def draw_middle_inverse(key, part):
    return draw_inverse(jax.random.fold_in(key, 13), MIDDLE)


def draw_top_inverse(key, part):
    return draw_inverse(jax.random.fold_in(key, 14), K3)


def draw_leaf_parent(key, part):
    chosen = jax.random.randint(jax.random.fold_in(key, 21), (LEAVES,), 0, PEERS)
    grid_row = jnp.arange(LEAVES, dtype=jnp.int32) // (LEAF_DEV * PEERS)
    return (grid_row * PEERS + chosen).astype(jnp.int32)


def draw_node_parent(key, part):
    chosen = jax.random.randint(jax.random.fold_in(key, 22), (NODES,), 0, K2)
    grid_row = jnp.arange(NODES, dtype=jnp.int32) // PEERS
    return (grid_row * K2 + chosen).astype(jnp.int32)


def set_ends(result, rng, least, largest):
    extent = result.shape
    place = [jax.random.randint(jax.random.fold_in(rng, axis), (), 0, extent[axis]) for axis in range(len(extent))]
    result = result.at[tuple(place)].set(least)
    longest = extent.index(max(extent))
    place[longest] = (place[longest] + 1) % extent[longest]
    return result.at[tuple(place)].set(largest)


def levels(stream_key, dims, cuts, smallest, top_value):
    level, own = 1.0, jax.random.fold_in(stream_key, 6)
    for axis_at, blocks in cuts:
        steps = jnp.exp(jax.random.uniform(jax.random.fold_in(own, axis_at), (blocks,), jnp.float32, smallest / len(cuts), top_value / len(cuts)))
        level = level * jnp.repeat(steps, dims[axis_at] // blocks).reshape([-1 if axis == axis_at else 1 for axis in range(len(dims))])
    return level


def centred(rng, shape, scale, most, cuts=(), held_as=jnp.bfloat16):
    level = levels(rng, shape, cuts, -0.22, 0.18) if cuts else 1.0
    values = jax.random.normal(rng, shape, jnp.float32) * scale * level
    return jnp.minimum(jnp.maximum(values, -most), most).astype(held_as)


def setup_inputs(seed: int = 0) -> dict:
    arg_keys = jax.random.split(jax.random.key(seed), 15)
    leaf_rhs = centred(arg_keys[0], (LEAVES, W, R), 1.0, 6.0, ((0, 32),))
    leaf_inverse = draw_leaf_inverse(jax.random.fold_in(arg_keys[14], 71), 0)
    leaf_link = centred(arg_keys[2], (LEAVES, W, W), (W * LEAF_DEV) ** -0.5, 0.109375, ((0, 32),))
    leaf_parent = draw_leaf_parent(jax.random.fold_in(arg_keys[14], 71), 0)
    node_rhs = centred(arg_keys[4], (NODES, W, R), 1.0, 6.0, ((0, 32),))
    node_inverse = draw_node_inverse(jax.random.fold_in(arg_keys[14], 71), 0)
    node_link = centred(arg_keys[6], (NODES, W, W), (W * PEERS // K2) ** -0.5, 0.5, ((0, 32),))
    node_parent = draw_node_parent(jax.random.fold_in(arg_keys[14], 71), 0)
    middle_rhs = centred(arg_keys[8], (MIDDLE, W, R), 1.0, 6.0, ((0, 4),))
    middle_inverse = draw_middle_inverse(jax.random.fold_in(arg_keys[14], 71), 0)
    middle_link = centred(arg_keys[10], (MIDDLE, W, W), (W * MIDDLE // K3) ** -0.5, 0.1875, ((0, 4),))
    middle_parent = set_ends(jax.random.randint(arg_keys[11], (MIDDLE,), 0, K3), jax.random.fold_in(arg_keys[11], 1), 0, K3 - 1).astype(jnp.int32)
    top_rhs = centred(arg_keys[12], (K3, W, R), 1.0, 6.0)
    top_inverse = draw_top_inverse(jax.random.fold_in(arg_keys[14], 71), 0)
    return {"leaf_rhs": leaf_rhs, "leaf_inverse": leaf_inverse, "leaf_link": leaf_link, "leaf_parent": leaf_parent, "node_rhs": node_rhs, "node_inverse": node_inverse, "node_link": node_link, "node_parent": node_parent, "middle_rhs": middle_rhs, "middle_inverse": middle_inverse, "middle_link": middle_link, "middle_parent": middle_parent, "top_rhs": top_rhs, "top_inverse": top_inverse}


def apply_block(matrix, vectors):
    return jnp.einsum("nij,njr->nir", matrix.astype(jnp.float32), vectors.astype(jnp.float32), precision=lax.Precision.HIGHEST)


def apply_transposed(matrix, vectors):
    return jnp.einsum("nij,nir->njr", matrix.astype(jnp.float32), vectors.astype(jnp.float32), precision=lax.Precision.HIGHEST)


def reference(leaf_rhs, leaf_inverse, leaf_link, leaf_parent, node_rhs, node_inverse, node_link, node_parent, middle_rhs, middle_inverse, middle_link, middle_parent, top_rhs, top_inverse):
    blocks = leaf_rhs.shape[0] // LEAF_DEV
    width = leaf_rhs.shape[1]
    columns = leaf_rhs.shape[2]
    items = (leaf_rhs.reshape(blocks, LEAF_DEV, width, columns), leaf_inverse.reshape(blocks, LEAF_DEV, width, width), leaf_link.reshape(blocks, LEAF_DEV, width, width), leaf_parent.reshape(blocks, LEAF_DEV))

    def forward_block(total, item):
        rhs, inverse, link, parent = item
        solved = apply_block(inverse, rhs).astype(jnp.bfloat16)
        update = apply_block(link, solved)
        total = total + jax.ops.segment_sum(update, parent, num_segments=NODES)
        return total, solved

    start = jnp.zeros((NODES, width, columns), jnp.float32)
    node_sum, leaf_solved = lax.scan(forward_block, start, items)
    node_y = (node_rhs.astype(jnp.float32) - node_sum).astype(jnp.bfloat16)
    node_solved = apply_block(node_inverse, node_y).astype(jnp.bfloat16)
    middle_sum = jax.ops.segment_sum(apply_block(node_link, node_solved), node_parent, num_segments=MIDDLE)
    middle_y = (middle_rhs.astype(jnp.float32) - middle_sum).astype(jnp.bfloat16)
    middle_solved = apply_block(middle_inverse, middle_y).astype(jnp.bfloat16)
    top_sum = jax.ops.segment_sum(apply_block(middle_link, middle_solved), middle_parent, num_segments=K3)
    top_y = (top_rhs.astype(jnp.float32) - top_sum).astype(jnp.bfloat16)
    top_solved = apply_block(top_inverse, top_y).astype(jnp.bfloat16)
    top_result = apply_transposed(top_inverse, top_solved).astype(jnp.bfloat16)
    middle_w = (middle_solved.astype(jnp.float32) - apply_transposed(middle_link, top_result[middle_parent])).astype(jnp.bfloat16)
    middle_result = apply_transposed(middle_inverse, middle_w).astype(jnp.bfloat16)
    node_w = (node_solved.astype(jnp.float32) - apply_transposed(node_link, middle_result[node_parent])).astype(jnp.bfloat16)
    node_result = apply_transposed(node_inverse, node_w).astype(jnp.bfloat16)

    def backward_block(item):
        solved, inverse, link, parent = item
        leaf_w = (solved.astype(jnp.float32) - apply_transposed(link, node_result[parent])).astype(jnp.bfloat16)
        return apply_transposed(inverse, leaf_w).astype(jnp.bfloat16)

    leaf_out = lax.map(backward_block, (leaf_solved, items[1], items[2], items[3]))
    leaf_result = leaf_out.reshape(blocks * LEAF_DEV, width, columns)
    return (leaf_result, node_result, middle_result, top_result)
```

```python
import functools

import jax
import jax.numpy as jnp
from jax import lax
from jax.experimental import pallas as pl
from jax.experimental.pallas import tpu as pltpu
from jax.sharding import PartitionSpec as P

MESH = pl.DeviceIdType.MESH
F32 = jnp.float32
BF16 = jnp.bfloat16
VMEM_LIMIT = 56 * 1024 * 1024


def mul(a, b):
    return jnp.dot(a, b, preferred_element_type=F32)


def mul_t(a, b):
    return lax.dot_general(a, b, (((0,), (0,)), ((), ())), preferred_element_type=F32)


def leaf_forward_kernel(steps, block, peers, target, rhs, inverse, link, solved, sums, total):
    step = pl.program_id(0)

    @pl.when(step == 0)
    def _():
        total[...] = jnp.zeros_like(total)

    for i in range(block):
        part = mul(inverse[i], rhs[i]).astype(BF16)
        solved[i] = part
        slot = target[step * block + i] % peers
        total[slot] += mul(link[i], part)

    @pl.when(step == steps - 1)
    def _():
        sums[...] = total[...].astype(BF16)


def leaf_backward_kernel(block, peers, target, solved, inverse, link, above, result):
    step = pl.program_id(0)
    for i in range(block):
        slot = target[step * block + i] % peers
        w = (solved[i].astype(F32) - mul_t(link[i], above[slot])).astype(BF16)
        result[i] = mul_t(inverse[i], w).astype(BF16)


def bits_of(index, count):
    return [(index // (1 << b)) % 2 for b in range(count)]


def log2(n):
    return n.bit_length() - 1


def tree_kernel(
    rows,
    peers,
    part,
    node_rhs,
    node_inverse,
    node_link,
    node_parent,
    middle_rhs,
    middle_inverse,
    middle_link,
    middle_parent,
    top_rhs,
    top_inverse,
    row_out,
    middle_out,
    top_out,
    work,
    landed,
    updates,
    choose,
    middle_solved,
    top_choose,
    top_term,
    top_landed,
    top_step,
    top_half,
    rs_send,
    rs_recv,
    up_send,
    up_recv,
    down_send,
    down_recv,
    row_send,
    row_recv,
):
    row, me = lax.axis_index("row"), lax.axis_index("col")
    width, columns = node_rhs.shape[1:]
    half = columns // 2
    halves = [slice(0, half), slice(half, columns)]
    middles, tops = middle_rhs.shape[0], top_rhs.shape[0]
    levels, row_levels = log2(peers), log2(rows)
    mine, row_mine = bits_of(me, levels), bits_of(row, row_levels)
    partner = [me + (1 - 2 * mine[b]) * (1 << b) for b in range(levels)]
    row_partner = [row + (1 - 2 * row_mine[b]) * (1 << b) for b in range(row_levels)]

    barrier = pltpu.get_barrier_semaphore()
    for p in partner:
        pl.semaphore_signal(barrier, inc=1, device_id=(row, p), device_id_type=MESH)
    for p in row_partner:
        pl.semaphore_signal(barrier, inc=1, device_id=(p, me), device_id_type=MESH)
    pl.semaphore_wait(barrier, levels + row_levels)

    first = list(range(levels))
    second = [1, 0] + first[2:] if levels > 1 else first
    orders = [first, second]
    pending = []

    def slot_of(flip):
        slot = 0
        for b in range(levels):
            bit = 1 - mine[b] if flip.get(b) else mine[b]
            slot = slot + bit * (1 << b)
        return slot

    def scatter_slot(h, k, j, sent):
        order = orders[h]
        free = order[k + 1 :]
        flip = {b: (j >> (len(free) - 1 - i)) & 1 for i, b in enumerate(free)}
        flip[order[k]] = sent
        return slot_of(flip)

    def scatter_place(k, j):
        return sum(1 << (levels - 1 - i) for i in range(k)) + j

    scatter = {}

    def scatter_start(h, k, j):
        slot = scatter_slot(h, k, j, 1)
        place = scatter_place(k, j)
        source = part if k == 0 else work
        copy = pltpu.make_async_remote_copy(
            src_ref=source.at[slot, :, halves[h]],
            dst_ref=landed.at[h, place],
            send_sem=rs_send.at[h, place],
            recv_sem=rs_recv.at[h, place],
            device_id=(row, partner[orders[h][k]]),
            device_id_type=MESH,
        )
        copy.start()
        scatter[h, k, j] = copy
        pending.append(copy)

    def scatter_add(h, k, j):
        scatter[h, k, j].wait_recv()
        slot = scatter_slot(h, k, j, 0)
        source = part if k == 0 else work
        return slot, source[slot, :, halves[h]].astype(F32) + landed[h, scatter_place(k, j)].astype(F32)

    for j in reversed(range(1 << (levels - 1))):
        for h in range(2):
            scatter_start(h, 0, j)

    eye = (
        lax.broadcasted_iota(jnp.int32, (width, width), 0) == lax.broadcasted_iota(jnp.int32, (width, width), 1)
    ).astype(F32)
    for c in range(peers):
        slot = node_parent[c] % middles
        for p in range(middles):
            choose[p, :, c * width : (c + 1) * width] = (eye * jnp.where(slot == p, 1.0, 0.0)).astype(BF16)
    for k in range(middles):
        slot = middle_parent[k]
        block = middle_link[k].astype(F32)
        for p in range(tops):
            top_choose[p, :, k * width : (k + 1) * width] = jnp.where(slot == p, block, 0.0).astype(BF16)

    for k in range(1, levels):
        count = 1 << (levels - 1 - k)
        for j in reversed(range(2 * count)):
            for h in range(2):
                slot, value = scatter_add(h, k - 1, j)
                work[slot, :, halves[h]] = value.astype(BF16)
                if j >= count:
                    scatter_start(h, k, j - count)

    def gather_slot(h, done, j):
        flip = {b: (j >> i) & 1 for i, b in enumerate(done)}
        return slot_of(flip)

    def gather_copy(buffer, send, recv, h, k, j):
        order = orders[h][::-1]
        slot = gather_slot(h, order[:k], j)
        place = (1 << k) - 1 + j
        view = buffer.at[slot, :, halves[h]]
        return pltpu.make_async_remote_copy(
            src_ref=view,
            dst_ref=view,
            send_sem=send.at[h, place],
            recv_sem=recv.at[h, place],
            device_id=(row, partner[order[k]]),
            device_id_type=MESH,
        )

    def gather_rest(buffer, send, recv, copies):
        for k in range(1, levels):
            for j in range(1 << k):
                for h in range(2):
                    old = 1 << (k - 1)
                    if j >= old:
                        copies[h, k - 1, j - old].wait_recv()
                    copy = gather_copy(buffer, send, recv, h, k, j)
                    copy.start()
                    copies[h, k, j] = copy
        for j in range(1 << (levels - 1)):
            for h in range(2):
                copies[h, levels - 1, j].wait_recv()
        pending.extend(copies.values())

    copies = {}
    node_solved = []
    for h in range(2):
        _, total = scatter_add(h, levels - 1, 0)
        node_y = (node_rhs[0, :, halves[h]].astype(F32) - total).astype(BF16)
        solved = mul(node_inverse[0], node_y).astype(BF16)
        updates[me, :, halves[h]] = mul(node_link[0], solved).astype(BF16)
        copies[h, 0, 0] = gather_copy(updates, up_send, up_recv, h, 0, 0)
        copies[h, 0, 0].start()
        node_solved.append(solved)
    gather_rest(updates, up_send, up_recv, copies)

    def middle_forward(p, carry):
        total = mul(choose[p], updates[...].reshape(peers * width, columns))
        middle_y = (middle_rhs[p].astype(F32) - total).astype(BF16)
        middle_solved[p] = mul(middle_inverse[p], middle_y).astype(BF16)
        return carry

    lax.fori_loop(0, middles, middle_forward, 0)

    for p in range(tops):
        total = mul(top_choose[p], middle_solved[...].reshape(middles * width, columns)).astype(BF16)
        for h in range(2):
            top_term[h, p] = total[:, halves[h]]

    core = row_mine[0]
    for k in range(row_levels):
        copy = pltpu.make_async_remote_copy(
            src_ref=top_term.at[1 - core] if k == 0 else top_step.at[k - 1],
            dst_ref=top_landed.at[k],
            send_sem=row_send.at[k],
            recv_sem=row_recv.at[k],
            device_id=(row_partner[k], me),
            device_id_type=MESH,
        )
        copy.start()
        pending.append(copy)
        copy.wait_recv()
        if k < row_levels - 1:
            held = top_term[core] if k == 0 else top_step[k - 1]
            top_step[k] = (held.astype(F32) + top_landed[k].astype(F32)).astype(BF16)
    for p in range(tops):
        last = row_levels - 1
        held = top_term[core, p] if last == 0 else top_step[last - 1, p]
        total = held.astype(F32) + top_landed[last, p].astype(F32)
        rhs = top_rhs[p].astype(F32)
        rhs = jnp.where(core == 0, rhs[:, :half], rhs[:, half:])
        solved = mul(top_inverse[p], (rhs - total).astype(BF16)).astype(BF16)
        top_half[core, p] = mul_t(top_inverse[p], solved).astype(BF16)
    view = top_half.at[core]
    copy = pltpu.make_async_remote_copy(
        src_ref=view,
        dst_ref=view,
        send_sem=row_send.at[row_levels],
        recv_sem=row_recv.at[row_levels],
        device_id=(row_partner[0], me),
        device_id_type=MESH,
    )
    copy.start()
    pending.append(copy)
    copy.wait_recv()
    for p in range(tops):
        for h in range(2):
            top_out[p, :, halves[h]] = top_half[h, p]

    def middle_backward(k):
        above = top_out[middle_parent[k]]
        w = (middle_solved[k].astype(F32) - mul_t(middle_link[k], above)).astype(BF16)
        return mul_t(middle_inverse[k], w).astype(BF16)

    own = middle_backward(node_parent[me] % middles)
    copies = {}
    for h in range(2):
        node_w = (node_solved[h].astype(F32) - mul_t(node_link[0], own[:, halves[h]])).astype(BF16)
        row_out[me, :, halves[h]] = mul_t(node_inverse[0], node_w).astype(BF16)
        copies[h, 0, 0] = gather_copy(row_out, down_send, down_recv, h, 0, 0)
        copies[h, 0, 0].start()

    def middle_store(k, carry):
        middle_out[k] = middle_backward(k)
        return carry

    lax.fori_loop(0, middles, middle_store, 0)
    gather_rest(row_out, down_send, down_recv, copies)
    for copy in pending:
        copy.wait_send()


def local(
    rows,
    peers,
    leaf_rhs,
    leaf_inverse,
    leaf_link,
    leaf_parent,
    node_rhs,
    node_inverse,
    node_link,
    node_parent,
    middle_rhs,
    middle_inverse,
    middle_link,
    middle_parent,
    top_rhs,
    top_inverse,
):
    leaves, width, columns = leaf_rhs.shape
    middles, tops = middle_rhs.shape[0], top_rhs.shape[0]
    half = columns // 2
    levels, row_levels = log2(peers), log2(rows)
    block = max(b for b in (1, 2, 3, 4) if leaves % b == 0)
    steps = leaves // block
    vectors = pl.BlockSpec((block, width, columns), lambda i, t: (i, 0, 0))
    matrices = pl.BlockSpec((block, width, width), lambda i, t: (i, 0, 0))
    slots = pl.BlockSpec((peers, width, columns), lambda i, t: (0, 0, 0))
    leaf_solved, sums = pl.pallas_call(
        functools.partial(leaf_forward_kernel, steps, block, peers),
        grid_spec=pltpu.PrefetchScalarGridSpec(
            num_scalar_prefetch=1,
            grid=(steps,),
            in_specs=[vectors, matrices, matrices],
            out_specs=[vectors, slots],
            scratch_shapes=[pltpu.VMEM((peers, width, columns), F32)],
        ),
        out_shape=[
            jax.ShapeDtypeStruct(leaf_rhs.shape, BF16),
            jax.ShapeDtypeStruct((peers, width, columns), BF16),
        ],
        compiler_params=pltpu.CompilerParams(vmem_limit_bytes=VMEM_LIMIT),
        name="leaf_forward",
    )(leaf_parent, leaf_rhs, leaf_inverse, leaf_link)

    vmem = pl.BlockSpec(memory_space=pltpu.VMEM)
    smem = pl.BlockSpec(memory_space=pltpu.SMEM)
    dma = pltpu.SemaphoreType.DMA
    row_result, middle_result, top_result = pl.pallas_call(
        functools.partial(tree_kernel, rows, peers),
        in_specs=[vmem] * 4 + [smem] + [vmem] * 3 + [smem] + [vmem] * 2,
        out_specs=[vmem] * 3,
        out_shape=[
            jax.ShapeDtypeStruct((peers, width, columns), BF16),
            jax.ShapeDtypeStruct(middle_rhs.shape, BF16),
            jax.ShapeDtypeStruct(top_rhs.shape, BF16),
        ],
        scratch_shapes=[
            pltpu.VMEM((peers, width, columns), BF16),
            pltpu.VMEM((2, peers - 1, width, half), BF16),
            pltpu.VMEM((peers, width, columns), BF16),
            pltpu.VMEM((middles, width, peers * width), BF16),
            pltpu.VMEM((middles, width, columns), BF16),
            pltpu.VMEM((tops, width, middles * width), BF16),
            pltpu.VMEM((2, tops, width, half), BF16),
            pltpu.VMEM((row_levels, tops, width, half), BF16),
            pltpu.VMEM((row_levels, tops, width, half), BF16),
            pltpu.VMEM((2, tops, width, half), BF16),
            dma((2, peers - 1)),
            dma((2, peers - 1)),
            dma((2, peers - 1)),
            dma((2, peers - 1)),
            dma((2, peers - 1)),
            dma((2, peers - 1)),
            dma((row_levels + 1,)),
            dma((row_levels + 1,)),
        ],
        compiler_params=pltpu.CompilerParams(
            collective_id=0, has_side_effects=True, vmem_limit_bytes=VMEM_LIMIT
        ),
        name="tree",
    )(
        sums,
        node_rhs,
        node_inverse,
        node_link,
        node_parent,
        middle_rhs,
        middle_inverse,
        middle_link,
        middle_parent,
        top_rhs,
        top_inverse,
    )
    node_result = lax.dynamic_slice_in_dim(row_result, lax.axis_index("col"), 1)

    leaf_result = pl.pallas_call(
        functools.partial(leaf_backward_kernel, block, peers),
        grid_spec=pltpu.PrefetchScalarGridSpec(
            num_scalar_prefetch=1,
            grid=(steps,),
            in_specs=[vectors, matrices, matrices, slots],
            out_specs=vectors,
        ),
        out_shape=jax.ShapeDtypeStruct(leaf_rhs.shape, BF16),
        compiler_params=pltpu.CompilerParams(vmem_limit_bytes=VMEM_LIMIT),
        name="leaf_backward",
    )(leaf_parent, leaf_solved, leaf_inverse, leaf_link, row_result)
    return (leaf_result, node_result, middle_result, top_result)


def solution(mesh):
    placed = (
        P(("row", "col"), None, None),
        P(("row", "col"), None, None),
        P(("row", "col"), None, None),
        P(("row", "col")),
        P(("row", "col"), None, None),
        P(("row", "col"), None, None),
        P(("row", "col"), None, None),
        P("row"),
        P("row", None, None),
        P("row", None, None),
        P("row", None, None),
        P("row"),
        P(),
        P(),
    )
    return jax.shard_map(
        functools.partial(local, mesh.shape["row"], mesh.shape["col"]),
        mesh=mesh,
        in_specs=placed,
        out_specs=(
            P(("row", "col"), None, None),
            P(("row", "col"), None, None),
            P("row", None, None),
            P(),
        ),
        check_vma=False,
    )
```

```python
import functools

import jax
import jax.numpy as jnp
from jax import lax
from jax.experimental import pallas as pl
from jax.experimental.pallas import tpu as pltpu
from jax.sharding import PartitionSpec as P

MESH = pl.DeviceIdType.MESH
F32 = jnp.float32
BF16 = jnp.bfloat16
VMEM_LIMIT = 56 * 1024 * 1024


def mul(a, b):
    return jnp.dot(a, b, preferred_element_type=F32)


def mul_t(a, b):
    return lax.dot_general(a, b, (((0,), (0,)), ((), ())), preferred_element_type=F32)


def leaf_forward_kernel(steps, block, peers, target, rhs, inverse, link, solved, sums, total):
    step = pl.program_id(0)

    @pl.when(step == 0)
    def _():
        total[...] = jnp.zeros_like(total)

    parts = [mul(inverse[i], rhs[i]).astype(BF16) for i in range(block)]
    for i in range(block):
        solved[i] = parts[i]
    updates = [mul(link[i], parts[i]) for i in range(block)]
    for i in range(block):
        slot = target[step * block + i] % peers
        total[slot] += updates[i]

    @pl.when(step == steps - 1)
    def _():
        sums[...] = total[...].astype(BF16)


def leaf_backward_kernel(
    steps, block, peers, target, solved, inverse, link, above, node, middle, top, result, node_out, middle_out, top_out, sem
):
    step = pl.program_id(0)
    pairs = [(node, node_out), (middle, middle_out), (top, top_out)]
    passed = [pltpu.make_async_copy(src, dst, sem.at[i]) for i, (src, dst) in enumerate(pairs)]

    @pl.when(step == 0)
    def _():
        for copy in passed:
            copy.start()

    parents = [above[target[step * block + i] % peers] for i in range(block)]
    w = [(solved[i].astype(F32) - mul_t(link[i], parents[i])).astype(BF16) for i in range(block)]
    results = [mul_t(inverse[i], w[i]).astype(BF16) for i in range(block)]
    for i in range(block):
        result[i] = results[i]

    @pl.when(step == steps - 1)
    def _():
        for copy in passed:
            copy.wait()


def bits_of(index, count):
    return [(index // (1 << b)) % 2 for b in range(count)]


def log2(n):
    return n.bit_length() - 1


def tree_kernel(
    rows,
    peers,
    part,
    node_rhs,
    node_inverse,
    node_link,
    node_parent,
    middle_rhs_hbm,
    middle_inverse_hbm,
    middle_link_hbm,
    middle_parent,
    top_rhs_hbm,
    top_inverse_hbm,
    row_out,
    node_out,
    middle_hbm,
    top_hbm,
    middle_rhs,
    middle_inverse,
    middle_link,
    top_rhs,
    top_inverse,
    middle_out,
    top_out,
    local_sem,
    work,
    landed,
    updates,
    choose,
    middle_solved,
    top_choose,
    top_term,
    top_landed,
    top_step,
    top_half,
    rs_send,
    rs_recv,
    up_send,
    up_recv,
    down_send,
    down_recv,
    row_send,
    row_recv,
):
    row, me = lax.axis_index("row"), lax.axis_index("col")
    width, columns = node_rhs.shape[1:]
    half = columns // 2
    halves = [slice(0, half), slice(half, columns)]
    middles, tops = middle_rhs.shape[0], top_rhs.shape[0]
    levels, row_levels = log2(peers), log2(rows)
    mine, row_mine = bits_of(me, levels), bits_of(row, row_levels)
    partner = [me + (1 - 2 * mine[b]) * (1 << b) for b in range(levels)]
    row_partner = [row + (1 - 2 * row_mine[b]) * (1 << b) for b in range(row_levels)]

    barrier = pltpu.get_barrier_semaphore()
    for p in partner:
        pl.semaphore_signal(barrier, inc=1, device_id=(row, p), device_id_type=MESH)
    for p in row_partner:
        pl.semaphore_signal(barrier, inc=1, device_id=(p, me), device_id_type=MESH)
    pl.semaphore_wait(barrier, levels + row_levels)

    first = list(range(levels))
    second = [1, 0] + first[2:] if levels > 1 else first
    orders = [first, second]
    pending = []

    def slot_of(flip):
        slot = 0
        for b in range(levels):
            bit = 1 - mine[b] if flip.get(b) else mine[b]
            slot = slot + bit * (1 << b)
        return slot

    def scatter_slot(h, k, j, sent):
        order = orders[h]
        free = order[k + 1 :]
        flip = {b: (j >> (len(free) - 1 - i)) & 1 for i, b in enumerate(free)}
        flip[order[k]] = sent
        return slot_of(flip)

    def scatter_place(k, j):
        return sum(1 << (levels - 1 - i) for i in range(k)) + j

    scatter = {}

    def scatter_start(h, k, j):
        slot = scatter_slot(h, k, j, 1)
        place = scatter_place(k, j)
        source = part if k == 0 else work
        copy = pltpu.make_async_remote_copy(
            src_ref=source.at[slot, :, halves[h]],
            dst_ref=landed.at[h, place],
            send_sem=rs_send.at[h, place],
            recv_sem=rs_recv.at[h, place],
            device_id=(row, partner[orders[h][k]]),
            device_id_type=MESH,
        )
        copy.start()
        scatter[h, k, j] = copy
        pending.append(copy)

    def scatter_add(h, k, j):
        scatter[h, k, j].wait_recv()
        slot = scatter_slot(h, k, j, 0)
        source = part if k == 0 else work
        return slot, source[slot, :, halves[h]].astype(F32) + landed[h, scatter_place(k, j)].astype(F32)

    for j in reversed(range(1 << (levels - 1))):
        for h in range(2):
            scatter_start(h, 0, j)

    sources = [middle_link_hbm, middle_inverse_hbm, middle_rhs_hbm, top_rhs_hbm, top_inverse_hbm]
    places = [middle_link, middle_inverse, middle_rhs, top_rhs, top_inverse]
    fetched = [pltpu.make_async_copy(sources[i], places[i], local_sem.at[i]) for i in range(5)]
    for copy in fetched:
        copy.start()

    eye = (
        lax.broadcasted_iota(jnp.int32, (width, width), 0) == lax.broadcasted_iota(jnp.int32, (width, width), 1)
    ).astype(F32)
    for c in range(peers):
        slot = node_parent[c] % middles
        for p in range(middles):
            choose[p * width : (p + 1) * width, c * width : (c + 1) * width] = (eye * jnp.where(slot == p, 1.0, 0.0)).astype(BF16)
    fetched[0].wait()
    for k in range(middles):
        slot = middle_parent[k]
        block = middle_link[k].astype(F32)
        for p in range(tops):
            top_choose[p * width : (p + 1) * width, k * width : (k + 1) * width] = jnp.where(slot == p, block, 0.0).astype(BF16)
    for copy in fetched[1:]:
        copy.wait()

    for k in range(1, levels):
        count = 1 << (levels - 1 - k)
        for j in reversed(range(2 * count)):
            for h in range(2):
                slot, value = scatter_add(h, k - 1, j)
                work[slot, :, halves[h]] = value.astype(BF16)
                if j >= count:
                    scatter_start(h, k, j - count)

    def gather_slot(h, done, j):
        flip = {b: (j >> i) & 1 for i, b in enumerate(done)}
        return slot_of(flip)

    def gather_copy(buffer, send, recv, h, k, j):
        order = orders[h][::-1]
        slot = gather_slot(h, order[:k], j)
        place = (1 << k) - 1 + j
        view = buffer.at[slot, :, halves[h]]
        return pltpu.make_async_remote_copy(
            src_ref=view,
            dst_ref=view,
            send_sem=send.at[h, place],
            recv_sem=recv.at[h, place],
            device_id=(row, partner[order[k]]),
            device_id_type=MESH,
        )

    def gather_forward(buffer, send, recv, copies, h, k, j):
        for later in range(k, levels):
            copy = gather_copy(buffer, send, recv, h, later, j)
            copy.start()
            copies[h, later, j] = copy

    def gather_level(buffer, send, recv, copies, k):
        for j in range(1 << k):
            for h in range(2):
                copies[h, k, j].wait_recv()
                gather_forward(buffer, send, recv, copies, h, k + 1, j + (1 << k))

    copies = {}
    node_solved = []
    for h in range(2):
        _, total = scatter_add(h, levels - 1, 0)
        node_y = (node_rhs[0, :, halves[h]].astype(F32) - total).astype(BF16)
        solved = mul(node_inverse[0], node_y).astype(BF16)
        updates[me, :, halves[h]] = mul(node_link[0], solved).astype(BF16)
        gather_forward(updates, up_send, up_recv, copies, h, 0, 0)
        node_solved.append(solved)
    for k in range(levels):
        gather_level(updates, up_send, up_recv, copies, k)
    pending.extend(copies.values())

    gathered = updates[...].reshape(peers * width, columns)
    group = max(g for g in (1, 2, 4) if middles % g == 0)
    for start in range(0, middles, group):
        total = mul(choose[start * width : (start + group) * width], gathered)
        for i in range(group):
            p = start + i
            middle_y = (middle_rhs[p].astype(F32) - total[i * width : (i + 1) * width]).astype(BF16)
            middle_solved[p] = mul(middle_inverse[p], middle_y).astype(BF16)

    core = row_mine[0]
    last = row_levels - 1

    def row_start(source, target, k, p, to):
        copy = pltpu.make_async_remote_copy(
            src_ref=source,
            dst_ref=target,
            send_sem=row_send.at[k, p],
            recv_sem=row_recv.at[k, p],
            device_id=(row_partner[to], me),
            device_id_type=MESH,
        )
        copy.start()
        pending.append(copy)
        return copy

    under = middle_solved[...].reshape(middles * width, columns)
    group = max(g for g in (1, 2) if tops % g == 0)
    sent = []
    for start in range(0, tops, group):
        total = mul(top_choose[start * width : (start + group) * width], under).astype(BF16)
        for i in range(group):
            p = start + i
            for h in range(2):
                top_term[h, p] = total[i * width : (i + 1) * width, halves[h]]
            sent.append(row_start(top_term.at[1 - core, p], top_landed.at[0, p], 0, p, 0))

    def row_sum(k, p):
        held = top_term[core, p] if k == 0 else top_step[k - 1, p]
        return held.astype(F32) + top_landed[k, p].astype(F32)

    for k in range(last):
        for p in range(tops):
            sent[p].wait_recv()
            top_step[k, p] = row_sum(k, p).astype(BF16)
            sent[p] = row_start(top_step.at[k, p], top_landed.at[k + 1, p], k + 1, p, k + 1)
    for p in range(tops):
        sent[p].wait_recv()
        rhs = top_rhs[p].astype(F32)
        rhs = jnp.where(core == 0, rhs[:, :half], rhs[:, half:])
        solved = mul(top_inverse[p], (rhs - row_sum(last, p)).astype(BF16)).astype(BF16)
        top_half[core, p] = mul_t(top_inverse[p], solved).astype(BF16)
        view = top_half.at[core, p]
        sent[p] = row_start(view, view, row_levels, p, 0)
    for p in range(tops):
        sent[p].wait_recv()
        for h in range(2):
            top_out[p, :, halves[h]] = top_half[h, p]
    stores = [pltpu.make_async_copy(top_out, top_hbm, local_sem.at[5])]
    stores[0].start()

    def middle_backward(k):
        above = top_out[middle_parent[k]]
        w = (middle_solved[k].astype(F32) - mul_t(middle_link[k], above)).astype(BF16)
        return mul_t(middle_inverse[k], w).astype(BF16)

    own = middle_backward(node_parent[me] % middles)
    copies = {}
    for h in range(2):
        node_w = (node_solved[h].astype(F32) - mul_t(node_link[0], own[:, halves[h]])).astype(BF16)
        node_result = mul_t(node_inverse[0], node_w).astype(BF16)
        row_out[me, :, halves[h]] = node_result
        gather_forward(row_out, down_send, down_recv, copies, h, 0, 0)
        node_out[0, :, halves[h]] = node_result

    def middle_store(ks):
        w = [(middle_solved[k].astype(F32) - mul_t(middle_link[k], top_out[middle_parent[k]])).astype(BF16) for k in ks]
        results = [mul_t(middle_inverse[k], w[i]).astype(BF16) for i, k in enumerate(ks)]
        for i, k in enumerate(ks):
            middle_out[k] = results[i]

    middle_store(range(middles // 2))
    for k in range(levels - 1):
        gather_level(row_out, down_send, down_recv, copies, k)
    middle_store(range(middles // 2, middles))
    stores.append(pltpu.make_async_copy(middle_out, middle_hbm, local_sem.at[6]))
    stores[1].start()
    gather_level(row_out, down_send, down_recv, copies, levels - 1)
    pending.extend(copies.values())
    for copy in pending:
        copy.wait_send()
    for copy in stores:
        copy.wait()


def local(
    rows,
    peers,
    leaf_rhs,
    leaf_inverse,
    leaf_link,
    leaf_parent,
    node_rhs,
    node_inverse,
    node_link,
    node_parent,
    middle_rhs,
    middle_inverse,
    middle_link,
    middle_parent,
    top_rhs,
    top_inverse,
):
    leaves, width, columns = leaf_rhs.shape
    middles, tops = middle_rhs.shape[0], top_rhs.shape[0]
    half = columns // 2
    levels, row_levels = log2(peers), log2(rows)
    block = max(b for b in (1, 2, 3, 4, 6) if leaves % b == 0)
    steps = leaves // block
    vectors = pl.BlockSpec((block, width, columns), lambda i, t: (i, 0, 0))
    matrices = pl.BlockSpec((block, width, width), lambda i, t: (i, 0, 0))
    slots = pl.BlockSpec((peers, width, columns), lambda i, t: (0, 0, 0))
    leaf_solved, sums = pl.pallas_call(
        functools.partial(leaf_forward_kernel, steps, block, peers),
        grid_spec=pltpu.PrefetchScalarGridSpec(
            num_scalar_prefetch=1,
            grid=(steps,),
            in_specs=[vectors, matrices, matrices],
            out_specs=[vectors, slots],
            scratch_shapes=[pltpu.VMEM((peers, width, columns), F32)],
        ),
        out_shape=[
            jax.ShapeDtypeStruct(leaf_rhs.shape, BF16),
            jax.ShapeDtypeStruct((peers, width, columns), BF16),
        ],
        compiler_params=pltpu.CompilerParams(vmem_limit_bytes=VMEM_LIMIT),
        name="leaf_forward",
    )(leaf_parent, leaf_rhs, leaf_inverse, leaf_link)

    vmem = pl.BlockSpec(memory_space=pltpu.VMEM)
    smem = pl.BlockSpec(memory_space=pltpu.SMEM)
    dma = pltpu.SemaphoreType.DMA
    anywhere = pl.BlockSpec(memory_space=pl.ANY)
    row_result, node_result, middle_result, top_result = pl.pallas_call(
        functools.partial(tree_kernel, rows, peers),
        in_specs=[vmem] * 4 + [smem] + [anywhere] * 3 + [smem] + [anywhere] * 2,
        out_specs=[vmem] * 2 + [anywhere] * 2,
        out_shape=[
            jax.ShapeDtypeStruct((peers, width, columns), BF16),
            jax.ShapeDtypeStruct(node_rhs.shape, BF16),
            jax.ShapeDtypeStruct(middle_rhs.shape, BF16),
            jax.ShapeDtypeStruct(top_rhs.shape, BF16),
        ],
        scratch_shapes=[
            pltpu.VMEM(middle_rhs.shape, BF16),
            pltpu.VMEM(middle_inverse.shape, BF16),
            pltpu.VMEM(middle_link.shape, BF16),
            pltpu.VMEM(top_rhs.shape, BF16),
            pltpu.VMEM(top_inverse.shape, BF16),
            pltpu.VMEM(middle_rhs.shape, BF16),
            pltpu.VMEM(top_rhs.shape, BF16),
            dma((7,)),
            pltpu.VMEM((peers, width, columns), BF16),
            pltpu.VMEM((2, peers - 1, width, half), BF16),
            pltpu.VMEM((peers, width, columns), BF16),
            pltpu.VMEM((middles * width, peers * width), BF16),
            pltpu.VMEM((middles, width, columns), BF16),
            pltpu.VMEM((tops * width, middles * width), BF16),
            pltpu.VMEM((2, tops, width, half), BF16),
            pltpu.VMEM((row_levels, tops, width, half), BF16),
            pltpu.VMEM((row_levels, tops, width, half), BF16),
            pltpu.VMEM((2, tops, width, half), BF16),
            dma((2, peers - 1)),
            dma((2, peers - 1)),
            dma((2, peers - 1)),
            dma((2, peers - 1)),
            dma((2, peers - 1)),
            dma((2, peers - 1)),
            dma((row_levels + 1, tops)),
            dma((row_levels + 1, tops)),
        ],
        compiler_params=pltpu.CompilerParams(
            collective_id=0, has_side_effects=True, vmem_limit_bytes=VMEM_LIMIT
        ),
        name="tree",
    )(
        sums,
        node_rhs,
        node_inverse,
        node_link,
        node_parent,
        middle_rhs,
        middle_inverse,
        middle_link,
        middle_parent,
        top_rhs,
        top_inverse,
    )

    leaf_result, node_result, middle_result, top_result = pl.pallas_call(
        functools.partial(leaf_backward_kernel, steps, block, peers),
        grid_spec=pltpu.PrefetchScalarGridSpec(
            num_scalar_prefetch=1,
            grid=(steps,),
            in_specs=[vectors, matrices, matrices, slots] + [anywhere] * 3,
            out_specs=[vectors] + [anywhere] * 3,
            scratch_shapes=[dma((3,))],
        ),
        out_shape=[jax.ShapeDtypeStruct(a.shape, BF16) for a in (leaf_rhs, node_rhs, middle_rhs, top_rhs)],
        compiler_params=pltpu.CompilerParams(vmem_limit_bytes=VMEM_LIMIT),
        name="leaf_backward",
    )(leaf_parent, leaf_solved, leaf_inverse, leaf_link, row_result, node_result, middle_result, top_result)
    return (leaf_result, node_result, middle_result, top_result)


def solution(mesh):
    placed = (
        P(("row", "col"), None, None),
        P(("row", "col"), None, None),
        P(("row", "col"), None, None),
        P(("row", "col")),
        P(("row", "col"), None, None),
        P(("row", "col"), None, None),
        P(("row", "col"), None, None),
        P("row"),
        P("row", None, None),
        P("row", None, None),
        P("row", None, None),
        P("row"),
        P(),
        P(),
    )
    return jax.shard_map(
        functools.partial(local, mesh.shape["row"], mesh.shape["col"]),
        mesh=mesh,
        in_specs=placed,
        out_specs=(
            P(("row", "col"), None, None),
            P(("row", "col"), None, None),
            P("row", None, None),
            P(),
        ),
        check_vma=False,
    )
```

```python
import functools

import jax
import jax.numpy as jnp
from jax import lax
from jax.experimental import pallas as pl
from jax.experimental.pallas import tpu as pltpu
from jax.sharding import PartitionSpec as P

MESH = pl.DeviceIdType.MESH
F32 = jnp.float32
BF16 = jnp.bfloat16
VMEM_LIMIT = 56 * 1024 * 1024


def mul(a, b):
    return jnp.dot(a, b, preferred_element_type=F32)


def mul_t(a, b):
    return lax.dot_general(a, b, (((0,), (0,)), ((), ())), preferred_element_type=F32)


def leaf_forward_kernel(steps, block, peers, target, rhs, inverse, link, solved, sums, total):
    step = pl.program_id(0)

    @pl.when(step == 0)
    def _():
        total[...] = jnp.zeros_like(total)

    parts = [mul(inverse[i], rhs[i]).astype(BF16) for i in range(block)]
    for i in range(block):
        solved[i] = parts[i]
    updates = [mul(link[i], parts[i]) for i in range(block)]
    for i in range(block):
        slot = target[step * block + i] % peers
        total[slot] += updates[i]

    @pl.when(step == steps - 1)
    def _():
        sums[...] = total[...].astype(BF16)


def leaf_backward_kernel(
    steps, block, peers, target, solved, inverse, link, above, node, middle, top, result, node_out, middle_out, top_out
):
    step = pl.program_id(0)
    middle_out[...] = middle[...]
    top_out[...] = top[...]

    @pl.when(step == 0)
    def _():
        node_out[...] = node[...]

    parents = [above[target[step * block + i] % peers] for i in range(block)]
    w = [(solved[i].astype(F32) - mul_t(link[i], parents[i])).astype(BF16) for i in range(block)]
    results = [mul_t(inverse[i], w[i]).astype(BF16) for i in range(block)]
    for i in range(block):
        result[i] = results[i]

def bits_of(index, count):
    return [(index // (1 << b)) % 2 for b in range(count)]


def log2(n):
    return n.bit_length() - 1


def tree_kernel(
    rows,
    peers,
    part,
    node_rhs,
    node_inverse,
    node_link,
    node_parent,
    middle_rhs_hbm,
    middle_inverse_hbm,
    middle_link_hbm,
    middle_parent,
    top_rhs_hbm,
    top_inverse_hbm,
    row_out,
    node_out,
    middle_hbm,
    top_hbm,
    middle_rhs,
    middle_inverse,
    middle_link,
    top_rhs,
    top_inverse,
    middle_out,
    top_out,
    local_sem,
    work,
    landed,
    updates,
    choose,
    middle_solved,
    top_choose,
    top_term,
    top_landed,
    top_step,
    top_half,
    rs_send,
    rs_recv,
    up_send,
    up_recv,
    down_send,
    down_recv,
    row_send,
    row_recv,
):
    row, me = lax.axis_index("row"), lax.axis_index("col")
    width, columns = node_rhs.shape[1:]
    half = columns // 2
    halves = [slice(0, half), slice(half, columns)]
    middles, tops = middle_rhs.shape[0], top_rhs.shape[0]
    levels, row_levels = log2(peers), log2(rows)
    mine, row_mine = bits_of(me, levels), bits_of(row, row_levels)
    partner = [me + (1 - 2 * mine[b]) * (1 << b) for b in range(levels)]
    row_partner = [row + (1 - 2 * row_mine[b]) * (1 << b) for b in range(row_levels)]

    barrier = pltpu.get_barrier_semaphore()
    for p in partner:
        pl.semaphore_signal(barrier, inc=1, device_id=(row, p), device_id_type=MESH)
    for p in row_partner:
        pl.semaphore_signal(barrier, inc=1, device_id=(p, me), device_id_type=MESH)
    pl.semaphore_wait(barrier, levels + row_levels)

    first = list(range(levels))
    second = [1, 0] + first[2:] if levels > 1 else first
    orders = [first, second]
    pending = []

    def slot_of(flip):
        slot = 0
        for b in range(levels):
            bit = 1 - mine[b] if flip.get(b) else mine[b]
            slot = slot + bit * (1 << b)
        return slot

    def scatter_slot(h, k, j, sent):
        order = orders[h]
        free = order[k + 1 :]
        flip = {b: (j >> (len(free) - 1 - i)) & 1 for i, b in enumerate(free)}
        flip[order[k]] = sent
        return slot_of(flip)

    def scatter_place(k, j):
        return sum(1 << (levels - 1 - i) for i in range(k)) + j

    scatter = {}

    def scatter_start(h, k, j):
        slot = scatter_slot(h, k, j, 1)
        place = scatter_place(k, j)
        source = part if k == 0 else work
        copy = pltpu.make_async_remote_copy(
            src_ref=source.at[slot, :, halves[h]],
            dst_ref=landed.at[h, place],
            send_sem=rs_send.at[h, place],
            recv_sem=rs_recv.at[h, place],
            device_id=(row, partner[orders[h][k]]),
            device_id_type=MESH,
        )
        copy.start()
        scatter[h, k, j] = copy
        pending.append(copy)

    def scatter_add(h, k, j):
        scatter[h, k, j].wait_recv()
        slot = scatter_slot(h, k, j, 0)
        source = part if k == 0 else work
        return slot, source[slot, :, halves[h]].astype(F32) + landed[h, scatter_place(k, j)].astype(F32)

    for j in reversed(range(1 << (levels - 1))):
        for h in range(2):
            scatter_start(h, 0, j)

    sources = [middle_link_hbm, middle_inverse_hbm, middle_rhs_hbm, top_rhs_hbm, top_inverse_hbm]
    places = [middle_link, middle_inverse, middle_rhs, top_rhs, top_inverse]
    fetched = [pltpu.make_async_copy(sources[i], places[i], local_sem.at[i]) for i in range(5)]
    for copy in fetched:
        copy.start()

    eye = (
        lax.broadcasted_iota(jnp.int32, (width, width), 0) == lax.broadcasted_iota(jnp.int32, (width, width), 1)
    ).astype(F32)
    for c in range(peers):
        slot = node_parent[c] % middles
        for p in range(middles):
            choose[p * width : (p + 1) * width, c * width : (c + 1) * width] = (eye * jnp.where(slot == p, 1.0, 0.0)).astype(BF16)
    fetched[0].wait()
    for k in range(middles):
        slot = middle_parent[k]
        block = middle_link[k].astype(F32)
        for p in range(tops):
            top_choose[p * width : (p + 1) * width, k * width : (k + 1) * width] = jnp.where(slot == p, block, 0.0).astype(BF16)
    for copy in fetched[1:]:
        copy.wait()

    for k in range(1, levels):
        count = 1 << (levels - 1 - k)
        for j in reversed(range(2 * count)):
            for h in range(2):
                slot, value = scatter_add(h, k - 1, j)
                work[slot, :, halves[h]] = value.astype(BF16)
                if j >= count:
                    scatter_start(h, k, j - count)

    def gather_slot(h, done, j):
        flip = {b: (j >> i) & 1 for i, b in enumerate(done)}
        return slot_of(flip)

    def gather_copy(buffer, send, recv, h, k, j):
        order = orders[h][::-1]
        slot = gather_slot(h, order[:k], j)
        place = (1 << k) - 1 + j
        view = buffer.at[slot, :, halves[h]]
        return pltpu.make_async_remote_copy(
            src_ref=view,
            dst_ref=view,
            send_sem=send.at[h, place],
            recv_sem=recv.at[h, place],
            device_id=(row, partner[order[k]]),
            device_id_type=MESH,
        )

    def gather_forward(buffer, send, recv, copies, h, k, j):
        for later in range(k, levels):
            copy = gather_copy(buffer, send, recv, h, later, j)
            copy.start()
            copies[h, later, j] = copy

    def gather_level(buffer, send, recv, copies, k):
        for j in range(1 << k):
            for h in range(2):
                copies[h, k, j].wait_recv()
                gather_forward(buffer, send, recv, copies, h, k + 1, j + (1 << k))

    copies = {}
    node_solved = []
    for h in range(2):
        _, total = scatter_add(h, levels - 1, 0)
        node_y = (node_rhs[0, :, halves[h]].astype(F32) - total).astype(BF16)
        solved = mul(node_inverse[0], node_y).astype(BF16)
        updates[me, :, halves[h]] = mul(node_link[0], solved).astype(BF16)
        gather_forward(updates, up_send, up_recv, copies, h, 0, 0)
        node_solved.append(solved)
    for k in range(levels):
        gather_level(updates, up_send, up_recv, copies, k)
    pending.extend(copies.values())

    gathered = updates[...].reshape(peers * width, columns)
    group = max(g for g in (1, 2, 4) if middles % g == 0)
    for start in range(0, middles, group):
        total = mul(choose[start * width : (start + group) * width], gathered)
        for i in range(group):
            p = start + i
            middle_y = (middle_rhs[p].astype(F32) - total[i * width : (i + 1) * width]).astype(BF16)
            middle_solved[p] = mul(middle_inverse[p], middle_y).astype(BF16)

    core = row_mine[0]
    last = row_levels - 1

    def row_start(source, target, k, p, to):
        copy = pltpu.make_async_remote_copy(
            src_ref=source,
            dst_ref=target,
            send_sem=row_send.at[k, p],
            recv_sem=row_recv.at[k, p],
            device_id=(row_partner[to], me),
            device_id_type=MESH,
        )
        copy.start()
        pending.append(copy)
        return copy

    under = middle_solved[...].reshape(middles * width, columns)
    group = max(g for g in (1, 2) if tops % g == 0)
    sent = []
    for start in range(0, tops, group):
        total = mul(top_choose[start * width : (start + group) * width], under).astype(BF16)
        for i in range(group):
            p = start + i
            for h in range(2):
                top_term[h, p] = total[i * width : (i + 1) * width, halves[h]]
            sent.append(row_start(top_term.at[1 - core, p], top_landed.at[0, p], 0, p, 0))

    def row_sum(k, p):
        held = top_term[core, p] if k == 0 else top_step[k - 1, p]
        return held.astype(F32) + top_landed[k, p].astype(F32)

    for k in range(last):
        for p in range(tops):
            sent[p].wait_recv()
            top_step[k, p] = row_sum(k, p).astype(BF16)
            sent[p] = row_start(top_step.at[k, p], top_landed.at[k + 1, p], k + 1, p, k + 1)
    for p in range(tops):
        sent[p].wait_recv()
        rhs = top_rhs[p].astype(F32)
        rhs = jnp.where(core == 0, rhs[:, :half], rhs[:, half:])
        solved = mul(top_inverse[p], (rhs - row_sum(last, p)).astype(BF16)).astype(BF16)
        top_half[core, p] = mul_t(top_inverse[p], solved).astype(BF16)
        view = top_half.at[core, p]
        sent[p] = row_start(view, view, row_levels, p, 0)
    for p in range(tops):
        sent[p].wait_recv()
        for h in range(2):
            top_out[p, :, halves[h]] = top_half[h, p]
    stores = [pltpu.make_async_copy(top_out, top_hbm, local_sem.at[5])]
    stores[0].start()

    def middle_backward(k):
        above = top_out[middle_parent[k]]
        w = (middle_solved[k].astype(F32) - mul_t(middle_link[k], above)).astype(BF16)
        return mul_t(middle_inverse[k], w).astype(BF16)

    own = middle_backward(node_parent[me] % middles)
    copies = {}
    for h in range(2):
        node_w = (node_solved[h].astype(F32) - mul_t(node_link[0], own[:, halves[h]])).astype(BF16)
        node_result = mul_t(node_inverse[0], node_w).astype(BF16)
        row_out[me, :, halves[h]] = node_result
        gather_forward(row_out, down_send, down_recv, copies, h, 0, 0)
        node_out[0, :, halves[h]] = node_result

    def middle_store(ks):
        w = [(middle_solved[k].astype(F32) - mul_t(middle_link[k], top_out[middle_parent[k]])).astype(BF16) for k in ks]
        results = [mul_t(middle_inverse[k], w[i]).astype(BF16) for i, k in enumerate(ks)]
        for i, k in enumerate(ks):
            middle_out[k] = results[i]

    middle_store(range(middles // 2))
    for k in range(levels - 1):
        gather_level(row_out, down_send, down_recv, copies, k)
    middle_store(range(middles // 2, middles))
    stores.append(pltpu.make_async_copy(middle_out, middle_hbm, local_sem.at[6]))
    stores[1].start()
    gather_level(row_out, down_send, down_recv, copies, levels - 1)
    pending.extend(copies.values())
    for copy in pending:
        copy.wait_send()
    for copy in stores:
        copy.wait()


def local(
    rows,
    peers,
    leaf_rhs,
    leaf_inverse,
    leaf_link,
    leaf_parent,
    node_rhs,
    node_inverse,
    node_link,
    node_parent,
    middle_rhs,
    middle_inverse,
    middle_link,
    middle_parent,
    top_rhs,
    top_inverse,
):
    leaves, width, columns = leaf_rhs.shape
    middles, tops = middle_rhs.shape[0], top_rhs.shape[0]
    half = columns // 2
    levels, row_levels = log2(peers), log2(rows)
    block = max(b for b in (1, 2, 3, 4, 6) if leaves % b == 0)
    steps = leaves // block
    vectors = pl.BlockSpec((block, width, columns), lambda i, t: (i, 0, 0))
    matrices = pl.BlockSpec((block, width, width), lambda i, t: (i, 0, 0))
    slots = pl.BlockSpec((peers, width, columns), lambda i, t: (0, 0, 0))
    leaf_solved, sums = pl.pallas_call(
        functools.partial(leaf_forward_kernel, steps, block, peers),
        grid_spec=pltpu.PrefetchScalarGridSpec(
            num_scalar_prefetch=1,
            grid=(steps,),
            in_specs=[vectors, matrices, matrices],
            out_specs=[vectors, slots],
            scratch_shapes=[pltpu.VMEM((peers, width, columns), F32)],
        ),
        out_shape=[
            jax.ShapeDtypeStruct(leaf_rhs.shape, BF16),
            jax.ShapeDtypeStruct((peers, width, columns), BF16),
        ],
        compiler_params=pltpu.CompilerParams(vmem_limit_bytes=VMEM_LIMIT),
        name="leaf_forward",
    )(leaf_parent, leaf_rhs, leaf_inverse, leaf_link)

    vmem = pl.BlockSpec(memory_space=pltpu.VMEM)
    smem = pl.BlockSpec(memory_space=pltpu.SMEM)
    dma = pltpu.SemaphoreType.DMA
    anywhere = pl.BlockSpec(memory_space=pl.ANY)
    row_result, node_result, middle_result, top_result = pl.pallas_call(
        functools.partial(tree_kernel, rows, peers),
        in_specs=[vmem] * 4 + [smem] + [anywhere] * 3 + [smem] + [anywhere] * 2,
        out_specs=[vmem] * 2 + [anywhere] * 2,
        out_shape=[
            jax.ShapeDtypeStruct((peers, width, columns), BF16),
            jax.ShapeDtypeStruct(node_rhs.shape, BF16),
            jax.ShapeDtypeStruct(middle_rhs.shape, BF16),
            jax.ShapeDtypeStruct(top_rhs.shape, BF16),
        ],
        scratch_shapes=[
            pltpu.VMEM(middle_rhs.shape, BF16),
            pltpu.VMEM(middle_inverse.shape, BF16),
            pltpu.VMEM(middle_link.shape, BF16),
            pltpu.VMEM(top_rhs.shape, BF16),
            pltpu.VMEM(top_inverse.shape, BF16),
            pltpu.VMEM(middle_rhs.shape, BF16),
            pltpu.VMEM(top_rhs.shape, BF16),
            dma((7,)),
            pltpu.VMEM((peers, width, columns), BF16),
            pltpu.VMEM((2, peers - 1, width, half), BF16),
            pltpu.VMEM((peers, width, columns), BF16),
            pltpu.VMEM((middles * width, peers * width), BF16),
            pltpu.VMEM((middles, width, columns), BF16),
            pltpu.VMEM((tops * width, middles * width), BF16),
            pltpu.VMEM((2, tops, width, half), BF16),
            pltpu.VMEM((row_levels, tops, width, half), BF16),
            pltpu.VMEM((row_levels, tops, width, half), BF16),
            pltpu.VMEM((2, tops, width, half), BF16),
            dma((2, peers - 1)),
            dma((2, peers - 1)),
            dma((2, peers - 1)),
            dma((2, peers - 1)),
            dma((2, peers - 1)),
            dma((2, peers - 1)),
            dma((row_levels + 1, tops)),
            dma((row_levels + 1, tops)),
        ],
        compiler_params=pltpu.CompilerParams(
            collective_id=0, has_side_effects=True, vmem_limit_bytes=VMEM_LIMIT
        ),
        name="tree",
    )(
        sums,
        node_rhs,
        node_inverse,
        node_link,
        node_parent,
        middle_rhs,
        middle_inverse,
        middle_link,
        middle_parent,
        top_rhs,
        top_inverse,
    )

    passed = []
    for count in (1, middles, tops):
        if count % steps == 0:
            passed.append(pl.BlockSpec((count // steps, width, columns), lambda i, t: (i, 0, 0)))
        else:
            passed.append(pl.BlockSpec((count, width, columns), lambda i, t: (0, 0, 0)))
    leaf_result, node_result, middle_result, top_result = pl.pallas_call(
        functools.partial(leaf_backward_kernel, steps, block, peers),
        grid_spec=pltpu.PrefetchScalarGridSpec(
            num_scalar_prefetch=1,
            grid=(steps,),
            in_specs=[vectors, matrices, matrices, slots] + passed,
            out_specs=[vectors] + passed,
        ),
        out_shape=[jax.ShapeDtypeStruct(a.shape, BF16) for a in (leaf_rhs, node_rhs, middle_rhs, top_rhs)],
        compiler_params=pltpu.CompilerParams(vmem_limit_bytes=VMEM_LIMIT),
        name="leaf_backward",
    )(leaf_parent, leaf_solved, leaf_inverse, leaf_link, row_result, node_result, middle_result, top_result)
    return (leaf_result, node_result, middle_result, top_result)


def solution(mesh):
    placed = (
        P(("row", "col"), None, None),
        P(("row", "col"), None, None),
        P(("row", "col"), None, None),
        P(("row", "col")),
        P(("row", "col"), None, None),
        P(("row", "col"), None, None),
        P(("row", "col"), None, None),
        P("row"),
        P("row", None, None),
        P("row", None, None),
        P("row", None, None),
        P("row"),
        P(),
        P(),
    )
    return jax.shard_map(
        functools.partial(local, mesh.shape["row"], mesh.shape["col"]),
        mesh=mesh,
        in_specs=placed,
        out_specs=(
            P(("row", "col"), None, None),
            P(("row", "col"), None, None),
            P("row", None, None),
            P(),
        ),
        check_vma=False,
    )
```

```python
import functools

import jax
import jax.numpy as jnp
from jax import lax
from jax.experimental import pallas as pl
from jax.experimental.pallas import tpu as pltpu
from jax.sharding import PartitionSpec as P

MESH = pl.DeviceIdType.MESH
F32 = jnp.float32
BF16 = jnp.bfloat16
VMEM_LIMIT = 56 * 1024 * 1024


def mul(a, b):
    return jnp.dot(a, b, preferred_element_type=F32)


def mul_t(a, b):
    return lax.dot_general(a, b, (((0,), (0,)), ((), ())), preferred_element_type=F32)


def leaf_forward_kernel(steps, block, peers, target, rhs, inverse, link, solved, sums, total):
    step = pl.program_id(0)

    @pl.when(step == 0)
    def _():
        total[...] = jnp.zeros_like(total)

    parts = [mul(inverse[i], rhs[i]).astype(BF16) for i in range(block)]
    for i in range(block):
        solved[i] = parts[i]
    updates = [mul(link[i], parts[i]) for i in range(block)]
    for i in range(block):
        slot = target[step * block + i] % peers
        total[slot] += updates[i]

    @pl.when(step == steps - 1)
    def _():
        sums[...] = total[...].astype(BF16)


def leaf_backward_kernel(
    steps, block, peers, target, solved, inverse, link, above, node, middle, top, result, node_out, middle_out, top_out
):
    step = pl.program_id(0)
    middle_out[...] = middle[...]
    top_out[...] = top[...]

    @pl.when(step == 0)
    def _():
        node_out[...] = node[...]

    parents = [above[target[step * block + i] % peers] for i in range(block)]
    w = [(solved[i].astype(F32) - mul_t(link[i], parents[i])).astype(BF16) for i in range(block)]
    results = [mul_t(inverse[i], w[i]).astype(BF16) for i in range(block)]
    for i in range(block):
        result[i] = results[i]

def bits_of(index, count):
    return [(index // (1 << b)) % 2 for b in range(count)]


def log2(n):
    return n.bit_length() - 1


def tree_kernel(
    rows,
    peers,
    part,
    node_rhs,
    node_inverse,
    node_link,
    node_parent,
    middle_rhs_hbm,
    middle_inverse_hbm,
    middle_link_hbm,
    middle_parent,
    top_rhs_hbm,
    top_inverse_hbm,
    row_out,
    node_out,
    middle_hbm,
    top_hbm,
    middle_rhs,
    middle_inverse,
    middle_link,
    top_rhs,
    top_inverse,
    middle_out,
    top_out,
    local_sem,
    work,
    landed,
    updates,
    choose,
    middle_solved,
    top_choose,
    top_term,
    top_landed,
    top_step,
    top_half,
    rs_send,
    rs_recv,
    up_send,
    up_recv,
    down_send,
    down_recv,
    row_send,
    row_recv,
):
    row, me = lax.axis_index("row"), lax.axis_index("col")
    width, columns = node_rhs.shape[1:]
    half = columns // 2
    cut = columns * 3 // 4
    cuts = [slice(0, cut), slice(cut, columns)]
    halves = [slice(0, half), slice(half, columns)]
    middles, tops = middle_rhs.shape[0], top_rhs.shape[0]
    levels, row_levels = log2(peers), log2(rows)
    mine, row_mine = bits_of(me, levels), bits_of(row, row_levels)
    partner = [me + (1 - 2 * mine[b]) * (1 << b) for b in range(levels)]
    row_partner = [row + (1 - 2 * row_mine[b]) * (1 << b) for b in range(row_levels)]

    barrier = pltpu.get_barrier_semaphore()
    for p in partner:
        pl.semaphore_signal(barrier, inc=1, device_id=(row, p), device_id_type=MESH)
    for p in row_partner:
        pl.semaphore_signal(barrier, inc=1, device_id=(p, me), device_id_type=MESH)
    pl.semaphore_wait(barrier, levels + row_levels)

    first = list(range(levels))
    second = [1, 0] + first[2:] if levels > 1 else first
    orders = [first, second]
    pending = []

    def slot_of(flip):
        slot = 0
        for b in range(levels):
            bit = 1 - mine[b] if flip.get(b) else mine[b]
            slot = slot + bit * (1 << b)
        return slot

    def scatter_slot(h, k, j, sent):
        order = orders[h]
        free = order[k + 1 :]
        flip = {b: (j >> (len(free) - 1 - i)) & 1 for i, b in enumerate(free)}
        flip[order[k]] = sent
        return slot_of(flip)

    def scatter_place(k, j):
        return sum(1 << (levels - 1 - i) for i in range(k)) + j

    scatter = {}

    def scatter_start(h, k, j):
        slot = scatter_slot(h, k, j, 1)
        place = scatter_place(k, j)
        source = part if k == 0 else work
        copy = pltpu.make_async_remote_copy(
            src_ref=source.at[slot, :, cuts[h]],
            dst_ref=landed.at[place, :, cuts[h]],
            send_sem=rs_send.at[h, place],
            recv_sem=rs_recv.at[h, place],
            device_id=(row, partner[orders[h][k]]),
            device_id_type=MESH,
        )
        copy.start()
        scatter[h, k, j] = copy
        pending.append(copy)

    def scatter_add(h, k, j):
        scatter[h, k, j].wait_recv()
        slot = scatter_slot(h, k, j, 0)
        source = part if k == 0 else work
        return slot, source[slot, :, cuts[h]].astype(F32) + landed[scatter_place(k, j), :, cuts[h]].astype(F32)

    for j in reversed(range(1 << (levels - 1))):
        for h in range(2):
            scatter_start(h, 0, j)

    sources = [middle_link_hbm, middle_inverse_hbm, middle_rhs_hbm, top_rhs_hbm, top_inverse_hbm]
    places = [middle_link, middle_inverse, middle_rhs, top_rhs, top_inverse]
    fetched = [pltpu.make_async_copy(sources[i], places[i], local_sem.at[i]) for i in range(5)]
    for copy in fetched:
        copy.start()

    eye = (
        lax.broadcasted_iota(jnp.int32, (width, width), 0) == lax.broadcasted_iota(jnp.int32, (width, width), 1)
    ).astype(F32)
    for c in range(peers):
        slot = node_parent[c] % middles
        for p in range(middles):
            choose[p * width : (p + 1) * width, c * width : (c + 1) * width] = (eye * jnp.where(slot == p, 1.0, 0.0)).astype(BF16)
    fetched[0].wait()
    for k in range(middles):
        slot = middle_parent[k]
        block = middle_link[k].astype(F32)
        for p in range(tops):
            top_choose[p * width : (p + 1) * width, k * width : (k + 1) * width] = jnp.where(slot == p, block, 0.0).astype(BF16)
    for copy in fetched[1:]:
        copy.wait()

    for k in range(1, levels):
        count = 1 << (levels - 1 - k)
        for j in reversed(range(2 * count)):
            for h in range(2):
                slot, value = scatter_add(h, k - 1, j)
                work[slot, :, cuts[h]] = value.astype(BF16)
                if j >= count:
                    scatter_start(h, k, j - count)

    def gather_slot(h, done, j):
        flip = {b: (j >> i) & 1 for i, b in enumerate(done)}
        return slot_of(flip)

    def gather_copy(buffer, send, recv, h, k, j):
        order = orders[h][::-1]
        slot = gather_slot(h, order[:k], j)
        place = (1 << k) - 1 + j
        view = buffer.at[slot, :, cuts[h]]
        return pltpu.make_async_remote_copy(
            src_ref=view,
            dst_ref=view,
            send_sem=send.at[h, place],
            recv_sem=recv.at[h, place],
            device_id=(row, partner[order[k]]),
            device_id_type=MESH,
        )

    def gather_forward(buffer, send, recv, copies, h, k, j):
        for later in range(k, levels):
            copy = gather_copy(buffer, send, recv, h, later, j)
            copy.start()
            copies[h, later, j] = copy

    def gather_level(buffer, send, recv, copies, k):
        for j in range(1 << k):
            for h in range(2):
                copies[h, k, j].wait_recv()
                gather_forward(buffer, send, recv, copies, h, k + 1, j + (1 << k))

    copies = {}
    node_solved = []
    for h in range(2):
        _, total = scatter_add(h, levels - 1, 0)
        node_y = (node_rhs[0, :, cuts[h]].astype(F32) - total).astype(BF16)
        solved = mul(node_inverse[0], node_y).astype(BF16)
        updates[me, :, cuts[h]] = mul(node_link[0], solved).astype(BF16)
        gather_forward(updates, up_send, up_recv, copies, h, 0, 0)
        node_solved.append(solved)
    for k in range(levels):
        gather_level(updates, up_send, up_recv, copies, k)
    pending.extend(copies.values())

    gathered = updates[...].reshape(peers * width, columns)
    group = max(g for g in (1, 2, 4) if middles % g == 0)
    for start in range(0, middles, group):
        total = mul(choose[start * width : (start + group) * width], gathered)
        for i in range(group):
            p = start + i
            middle_y = (middle_rhs[p].astype(F32) - total[i * width : (i + 1) * width]).astype(BF16)
            middle_solved[p] = mul(middle_inverse[p], middle_y).astype(BF16)

    core = row_mine[0]
    last = row_levels - 1

    def row_start(source, target, k, p, to):
        copy = pltpu.make_async_remote_copy(
            src_ref=source,
            dst_ref=target,
            send_sem=row_send.at[k, p],
            recv_sem=row_recv.at[k, p],
            device_id=(row_partner[to], me),
            device_id_type=MESH,
        )
        copy.start()
        pending.append(copy)
        return copy

    under = middle_solved[...].reshape(middles * width, columns)
    group = max(g for g in (1, 2) if tops % g == 0)
    sent = []
    for start in range(0, tops, group):
        total = mul(top_choose[start * width : (start + group) * width], under).astype(BF16)
        for i in range(group):
            p = start + i
            for h in range(2):
                top_term[h, p] = total[i * width : (i + 1) * width, halves[h]]
            sent.append(row_start(top_term.at[1 - core, p], top_landed.at[0, p], 0, p, 0))

    def row_sum(k, p):
        held = top_term[core, p] if k == 0 else top_step[k - 1, p]
        return held.astype(F32) + top_landed[k, p].astype(F32)

    for k in range(last):
        for p in range(tops):
            sent[p].wait_recv()
            top_step[k, p] = row_sum(k, p).astype(BF16)
            sent[p] = row_start(top_step.at[k, p], top_landed.at[k + 1, p], k + 1, p, k + 1)
    for p in range(tops):
        sent[p].wait_recv()
        rhs = top_rhs[p].astype(F32)
        rhs = jnp.where(core == 0, rhs[:, :half], rhs[:, half:])
        solved = mul(top_inverse[p], (rhs - row_sum(last, p)).astype(BF16)).astype(BF16)
        top_half[core, p] = mul_t(top_inverse[p], solved).astype(BF16)
        view = top_half.at[core, p]
        sent[p] = row_start(view, view, row_levels, p, 0)
    for p in range(tops):
        sent[p].wait_recv()
        for h in range(2):
            top_out[p, :, halves[h]] = top_half[h, p]
    stores = [pltpu.make_async_copy(top_out, top_hbm, local_sem.at[5])]
    stores[0].start()

    def middle_backward(k):
        above = top_out[middle_parent[k]]
        w = (middle_solved[k].astype(F32) - mul_t(middle_link[k], above)).astype(BF16)
        return mul_t(middle_inverse[k], w).astype(BF16)

    own = middle_backward(node_parent[me] % middles)
    copies = {}
    for h in range(2):
        node_w = (node_solved[h].astype(F32) - mul_t(node_link[0], own[:, cuts[h]])).astype(BF16)
        node_result = mul_t(node_inverse[0], node_w).astype(BF16)
        row_out[me, :, cuts[h]] = node_result
        gather_forward(row_out, down_send, down_recv, copies, h, 0, 0)
        node_out[0, :, cuts[h]] = node_result

    def middle_store(ks):
        w = [(middle_solved[k].astype(F32) - mul_t(middle_link[k], top_out[middle_parent[k]])).astype(BF16) for k in ks]
        results = [mul_t(middle_inverse[k], w[i]).astype(BF16) for i, k in enumerate(ks)]
        for i, k in enumerate(ks):
            middle_out[k] = results[i]

    middle_store(range(middles // 2))
    for k in range(levels - 1):
        gather_level(row_out, down_send, down_recv, copies, k)
    middle_store(range(middles // 2, middles))
    stores.append(pltpu.make_async_copy(middle_out, middle_hbm, local_sem.at[6]))
    stores[1].start()
    gather_level(row_out, down_send, down_recv, copies, levels - 1)
    pending.extend(copies.values())
    for copy in pending:
        copy.wait_send()
    for copy in stores:
        copy.wait()


def local(
    rows,
    peers,
    leaf_rhs,
    leaf_inverse,
    leaf_link,
    leaf_parent,
    node_rhs,
    node_inverse,
    node_link,
    node_parent,
    middle_rhs,
    middle_inverse,
    middle_link,
    middle_parent,
    top_rhs,
    top_inverse,
):
    leaves, width, columns = leaf_rhs.shape
    middles, tops = middle_rhs.shape[0], top_rhs.shape[0]
    half = columns // 2
    levels, row_levels = log2(peers), log2(rows)
    block = max(b for b in (1, 2, 3, 4, 6) if leaves % b == 0)
    steps = leaves // block
    vectors = pl.BlockSpec((block, width, columns), lambda i, t: (i, 0, 0))
    matrices = pl.BlockSpec((block, width, width), lambda i, t: (i, 0, 0))
    slots = pl.BlockSpec((peers, width, columns), lambda i, t: (0, 0, 0))
    leaf_solved, sums = pl.pallas_call(
        functools.partial(leaf_forward_kernel, steps, block, peers),
        grid_spec=pltpu.PrefetchScalarGridSpec(
            num_scalar_prefetch=1,
            grid=(steps,),
            in_specs=[vectors, matrices, matrices],
            out_specs=[vectors, slots],
            scratch_shapes=[pltpu.VMEM((peers, width, columns), F32)],
        ),
        out_shape=[
            jax.ShapeDtypeStruct(leaf_rhs.shape, BF16),
            jax.ShapeDtypeStruct((peers, width, columns), BF16),
        ],
        compiler_params=pltpu.CompilerParams(vmem_limit_bytes=VMEM_LIMIT),
        name="leaf_forward",
    )(leaf_parent, leaf_rhs, leaf_inverse, leaf_link)

    vmem = pl.BlockSpec(memory_space=pltpu.VMEM)
    smem = pl.BlockSpec(memory_space=pltpu.SMEM)
    dma = pltpu.SemaphoreType.DMA
    anywhere = pl.BlockSpec(memory_space=pl.ANY)
    row_result, node_result, middle_result, top_result = pl.pallas_call(
        functools.partial(tree_kernel, rows, peers),
        in_specs=[vmem] * 4 + [smem] + [anywhere] * 3 + [smem] + [anywhere] * 2,
        out_specs=[vmem] * 2 + [anywhere] * 2,
        out_shape=[
            jax.ShapeDtypeStruct((peers, width, columns), BF16),
            jax.ShapeDtypeStruct(node_rhs.shape, BF16),
            jax.ShapeDtypeStruct(middle_rhs.shape, BF16),
            jax.ShapeDtypeStruct(top_rhs.shape, BF16),
        ],
        scratch_shapes=[
            pltpu.VMEM(middle_rhs.shape, BF16),
            pltpu.VMEM(middle_inverse.shape, BF16),
            pltpu.VMEM(middle_link.shape, BF16),
            pltpu.VMEM(top_rhs.shape, BF16),
            pltpu.VMEM(top_inverse.shape, BF16),
            pltpu.VMEM(middle_rhs.shape, BF16),
            pltpu.VMEM(top_rhs.shape, BF16),
            dma((7,)),
            pltpu.VMEM((peers, width, columns), BF16),
            pltpu.VMEM((peers - 1, width, columns), BF16),
            pltpu.VMEM((peers, width, columns), BF16),
            pltpu.VMEM((middles * width, peers * width), BF16),
            pltpu.VMEM((middles, width, columns), BF16),
            pltpu.VMEM((tops * width, middles * width), BF16),
            pltpu.VMEM((2, tops, width, half), BF16),
            pltpu.VMEM((row_levels, tops, width, half), BF16),
            pltpu.VMEM((row_levels, tops, width, half), BF16),
            pltpu.VMEM((2, tops, width, half), BF16),
            dma((2, peers - 1)),
            dma((2, peers - 1)),
            dma((2, peers - 1)),
            dma((2, peers - 1)),
            dma((2, peers - 1)),
            dma((2, peers - 1)),
            dma((row_levels + 1, tops)),
            dma((row_levels + 1, tops)),
        ],
        compiler_params=pltpu.CompilerParams(
            collective_id=0, has_side_effects=True, vmem_limit_bytes=VMEM_LIMIT
        ),
        name="tree",
    )(
        sums,
        node_rhs,
        node_inverse,
        node_link,
        node_parent,
        middle_rhs,
        middle_inverse,
        middle_link,
        middle_parent,
        top_rhs,
        top_inverse,
    )

    passed = []
    for count in (1, middles, tops):
        if count % steps == 0:
            passed.append(pl.BlockSpec((count // steps, width, columns), lambda i, t: (i, 0, 0)))
        else:
            passed.append(pl.BlockSpec((count, width, columns), lambda i, t: (0, 0, 0)))
    leaf_result, node_result, middle_result, top_result = pl.pallas_call(
        functools.partial(leaf_backward_kernel, steps, block, peers),
        grid_spec=pltpu.PrefetchScalarGridSpec(
            num_scalar_prefetch=1,
            grid=(steps,),
            in_specs=[vectors, matrices, matrices, slots] + passed,
            out_specs=[vectors] + passed,
        ),
        out_shape=[jax.ShapeDtypeStruct(a.shape, BF16) for a in (leaf_rhs, node_rhs, middle_rhs, top_rhs)],
        compiler_params=pltpu.CompilerParams(vmem_limit_bytes=VMEM_LIMIT),
        name="leaf_backward",
    )(leaf_parent, leaf_solved, leaf_inverse, leaf_link, row_result, node_result, middle_result, top_result)
    return (leaf_result, node_result, middle_result, top_result)


def solution(mesh):
    placed = (
        P(("row", "col"), None, None),
        P(("row", "col"), None, None),
        P(("row", "col"), None, None),
        P(("row", "col")),
        P(("row", "col"), None, None),
        P(("row", "col"), None, None),
        P(("row", "col"), None, None),
        P("row"),
        P("row", None, None),
        P("row", None, None),
        P("row", None, None),
        P("row"),
        P(),
        P(),
    )
    return jax.shard_map(
        functools.partial(local, mesh.shape["row"], mesh.shape["col"]),
        mesh=mesh,
        in_specs=placed,
        out_specs=(
            P(("row", "col"), None, None),
            P(("row", "col"), None, None),
            P("row", None, None),
            P(),
        ),
        check_vma=False,
    )
```
